256 devices in a mesh: rep: 8 (over x, z_hi), fsdp: 32 (over z_lo, y, core).
Axes of the slice: x: 4, y: 4, z: 8 (z_hi: 2, z_lo: 4; z = z_hi * 4 + z_lo), core: 2. Of those that a mesh axis runs over, the one named last changes fastest.
Arguments:
- inputs: bfloat16 [32768, 8192], P(('rep', 'fsdp')), may hold values from -24 to 24
- cotangent: bfloat16 [32768, 512], P(('rep', 'fsdp')), may hold values from -6 to 6
- value_weight: bfloat16 [65536, 512], P(('rep', 'fsdp')), may hold values from -0.0625 to 0.0625
- norm_gain: float32 [65536], P('rep'), may hold values from 0.1 to 1.9
- outer_delta: float32 [65536, 1024], P(('rep', 'fsdp')), may hold values from -4 to 4
- outer_params: float32 [8192, 1024], P('fsdp', 'rep'), may hold values from -6 to 6
- outer_moment: float32 [8192, 1024], P('fsdp', 'rep'), may hold values from -4 to 4
Outputs:
- values: float32 [32768, 512], P(('rep', 'fsdp'))
- input_grad: float32 [32768, 8192], P(('rep', 'fsdp'))
- weight_grad: float32 [65536, 512], P(('rep', 'fsdp'))
- gain_grad: float32 [65536], P(('rep', 'fsdp'))
- new_params: float32 [8192, 1024], P('fsdp', 'rep')
- new_moment: float32 [8192, 1024], P('fsdp', 'rep')
The draws below stay inside these ranges and needn't reach their ends.
All inputs are finite; a program needn't handle non-finite values.
Results may differ from the reference program's by a relative error of at most 0.0029.
Values may be sent and summed in bfloat16 or wider, within the bound.
No kernel may reach another device: no remote copies, remote signals or barrier semaphores. Data moves between devices by JAX's collectives and lax.ppermute only.
A program may use at most 128 MiB of HBM per device.

```python
import math
import jax
import jax.numpy as jnp
from jax import lax

D = 8192
KF = 1024
KVW = 512
TOK_DEV = 128
TOKENS = 32768
N_REP = 8
N_FSDP = 32


def strengthened(array, key, source, target, parts, factor):
    owner, partner = [(jnp.arange(array.shape[axis_at]) // (array.shape[axis_at] // parts)).reshape([-1 if axis == axis_at else 1 for axis in range(array.ndim)]) for axis_at in (source, target)]
    chosen = jax.random.permutation(key, parts)[partner]
    strong = (owner == chosen) | (owner == (partner + parts // 2) % parts)
    return jnp.where(strong, factor * array, array)


def block_levels(stream_key, dims, split, low, high):
    level, own = 1.0, jax.random.fold_in(stream_key, 6)
    for dim, blocks in split:
        heights = jnp.exp(jax.random.uniform(jax.random.fold_in(own, dim), (blocks,), jnp.float32, low / len(split), high / len(split)))
        level = level * jnp.repeat(heights, dims[dim] // blocks).reshape([-1 if axis == dim else 1 for axis in range(len(dims))])
    return level


def bell_draw(stream_key, shape, deviation, reach, split=(), kind=jnp.bfloat16):
    result = jax.random.normal(stream_key, shape, jnp.float32) * deviation
    if len(split) > 0:
        result = block_levels(stream_key, shape, split, -0.22, 0.18) * result
    return jnp.clip(result, min=-reach, max=reach).astype(kind)


def bell_draw_with(own_key, dims, width, limit, cuts, heavy, dtype=jnp.bfloat16):
    array = width * jax.random.normal(own_key, dims, jnp.float32)
    if cuts:
        array = array * block_levels(own_key, dims, cuts, -0.22, 0.18)
    return jnp.clip(strengthened(array, jax.random.fold_in(own_key, 3), *heavy), -limit, limit).astype(dtype)


def setup_inputs(seed: int = 0) -> dict:
    splits = jax.random.split(jax.random.key(seed), 8)
    inputs = bell_draw_with(splits[0], (TOKENS, D), 1.0, 24.0, ((0, 256),), (0, 1, 256, 6.0))
    cotangent = bell_draw(splits[1], (TOKENS, KVW), 1.0, 6.0, ((0, 256),))
    value_weight = bell_draw(splits[2], (N_REP * D, KVW), D ** -0.5, 0.0625, ((0, 256),))
    norm_gain = jnp.clip(1.0 + 0.18 * jax.random.normal(splits[3], (N_REP * D,), jnp.float32), 0.1, 1.9)
    outer_delta = bell_draw(splits[4], (N_REP * D, KF), 0.5, 4.0, ((0, 256),), jnp.float32)
    outer_params = bell_draw(splits[5], (D, KF), 1.0, 6.0, ((0, 32), (1, 8)), jnp.float32)
    outer_moment = bell_draw(splits[6], (D, KF), 0.5, 4.0, ((0, 32), (1, 8)), jnp.float32)
    return {"inputs": inputs, "cotangent": cotangent, "value_weight": value_weight, "norm_gain": norm_gain, "outer_delta": outer_delta, "outer_params": outer_params, "outer_moment": outer_moment}


def one_group(pieces):
    inputs, cotangent, weight, gain = pieces
    scale_grad = 1.0 / math.sqrt(TOK_DEV * N_FSDP)
    floats = inputs.astype(jnp.float32)
    scale = lax.rsqrt(lax.optimization_barrier(jnp.mean(floats * floats, axis=-1, keepdims=True)) + 1e-05)
    normed = floats * scale
    hidden = (normed * gain).astype(jnp.bfloat16)
    values = jnp.dot(hidden, weight, preferred_element_type=jnp.float32)
    hidden_grad = lax.dot_general(cotangent, weight, (((1,), (1,)), ((), ())), preferred_element_type=jnp.float32)
    scaled = hidden_grad * gain
    input_grad = scale * (scaled - normed * lax.optimization_barrier(jnp.mean(scaled * normed, axis=-1, keepdims=True)))
    weight_sum = lax.dot_general(hidden, cotangent, (((0,), (0,)), ((), ())), preferred_element_type=jnp.float32)
    gain_sum = lax.optimization_barrier(jnp.sum(hidden_grad * normed, axis=0))
    return (values, input_grad, weight_sum * scale_grad, gain_sum * scale_grad)

def reference(inputs, cotangent, value_weight, norm_gain, outer_delta, outer_params, outer_moment):
    grouped = (inputs.reshape(N_REP, TOK_DEV * N_FSDP, D), cotangent.reshape(N_REP, TOK_DEV * N_FSDP, KVW), value_weight.reshape(N_REP, D, KVW), norm_gain.reshape(N_REP, D))
    values, input_grad, weight_grad, gain_grad = lax.map(one_group, grouped)
    average = lax.optimization_barrier(jnp.sum(outer_delta.reshape(N_REP, D, KF), axis=0)) / N_REP
    new_moment = 0.9 * outer_moment + average
    new_params = outer_params - 0.7 * (average + 0.9 * new_moment)
    return (values.reshape(TOKENS, KVW), input_grad.reshape(TOKENS, D), weight_grad.reshape(N_REP * D, KVW), gain_grad.reshape(N_REP * D), new_params, new_moment)
```

```python
import functools
import math

import jax
import jax.numpy as jnp
from jax import lax
from jax.experimental import pallas as pl
from jax.experimental.pallas import tpu as pltpu
from jax.sharding import PartitionSpec as P

F32 = jnp.float32
BF16 = jnp.bfloat16

NZ, NY, NC, NX = 4, 4, 2, 4
PLANE = NY * NC
OFFSETS = [(dy, dc) for dy in range(NY) for dc in range(NC)]
SENDS = [(1, 0), (3, 0), (1, 1), (3, 1), (2, 0), (2, 1), (0, 1)]


def split_index(index):
    return index // PLANE, (index // NC) % NY, index % NC


def fsdp_perm(dz, dy, dc):
    pairs = []
    for source in range(NZ * PLANE):
        z, y, c = split_index(source)
        target = ((z + dz) % NZ) * PLANE + ((y + dy) % NY) * NC + (c ^ dc)
        pairs.append((source, target))
    return pairs


def rep_perm(dx, dh):
    return [
        (x * 2 + h, ((x + dx) % NX) * 2 + (h ^ dh)) for x in range(NX) for h in range(2)
    ]


def send(array, dz=0, dy=0, dc=0):
    return lax.ppermute(array, "fsdp", fsdp_perm(dz % NZ, dy % NY, dc))


def vmem_params(mib=48):
    return pltpu.CompilerParams(vmem_limit_bytes=mib * 2**20)


def feature_start(position, dz, dy, dc, rows):
    z, y, c = position
    owner = ((z + dz) % NZ) * PLANE + ((y + dy) % NY) * NC + (c ^ dc)
    return pl.multiple_of(owner * rows, rows)


def norm_kernel(place, x_ref, gain_ref, scale_ref, *out_refs):
    position = (place[0], place[1], place[2])
    floats = x_ref[...].astype(F32)
    mean = jnp.mean(floats * floats, axis=-1, keepdims=True)
    scale = lax.rsqrt(mean + 1e-05)
    scale_ref[...] = scale
    rows = x_ref.shape[1] // (NZ * PLANE)
    for (dy, dc), out in zip(OFFSETS, out_refs):
        for dz in range(NZ):
            at = pl.ds(feature_start(position, dz, dy, dc, rows), rows)
            normed = x_ref[:, at].astype(F32) * scale
            out[:, dz * rows : (dz + 1) * rows] = (normed * gain_ref[:, at]).astype(BF16)


def make_hidden(place, inputs, gain):
    tokens, width = inputs.shape
    step = 32
    block = width // PLANE
    return pl.pallas_call(
        norm_kernel,
        grid=(tokens // step,),
        in_specs=[
            pl.BlockSpec(memory_space=pltpu.SMEM),
            pl.BlockSpec((step, width), lambda i: (i, 0)),
            pl.BlockSpec((1, width), lambda i: (0, 0)),
        ],
        out_specs=[pl.BlockSpec((step, 1), lambda i: (i, 0))]
        + [pl.BlockSpec((step, block), lambda i: (i, 0))] * PLANE,
        out_shape=[jax.ShapeDtypeStruct((tokens, 1), F32)]
        + [jax.ShapeDtypeStruct((tokens, block), BF16)] * PLANE,
        compiler_params=vmem_params(),
        cost_estimate=pl.CostEstimate(
            flops=6 * tokens * width, bytes_accessed=4 * tokens * width, transcendentals=0
        ),
        name="norm",
    )(place, inputs, gain)


def hidden_grad_kernel(*refs):
    cots, weights, outs = refs[:PLANE], refs[PLANE : PLANE + NZ], refs[PLANE + NZ :]
    for cot, out in zip(cots, outs):
        for dz, weight in enumerate(weights):
            rows = weight.shape[0]
            out[:, dz * rows : (dz + 1) * rows] = lax.dot_general(
                cot[...], weight[...], (((1,), (1,)), ((), ())), preferred_element_type=F32
            ).astype(BF16)


def make_hidden_grad(cots, weights):
    tokens, inner = cots[0].shape
    block = NZ * weights[0].shape[0]
    return pl.pallas_call(
        hidden_grad_kernel,
        out_shape=[jax.ShapeDtypeStruct((tokens, block), BF16)] * PLANE,
        compiler_params=vmem_params(),
        cost_estimate=pl.CostEstimate(
            flops=2 * PLANE * tokens * inner * block,
            bytes_accessed=2 * PLANE * tokens * (inner + block) + 2 * block * inner,
            transcendentals=0,
        ),
        name="hidden_grad",
    )(*cots, *weights)


def weight_kernel(*refs):
    hiddens, cots, outs = refs[:PLANE], refs[PLANE : 2 * PLANE], refs[2 * PLANE :]
    cot = jnp.concatenate([ref[...] for ref in cots], axis=0)
    rows = outs[0].shape[0]
    for dz, out in enumerate(outs):
        hidden = jnp.concatenate(
            [ref[:, dz * rows : (dz + 1) * rows] for ref in hiddens], axis=0
        )
        out[...] = lax.dot_general(
            hidden, cot, (((0,), (0,)), ((), ())), preferred_element_type=F32
        ).astype(out.dtype)


def make_weight_terms(hiddens, cots):
    tokens, block = hiddens[0].shape
    inner = cots[0].shape[1]
    rows = block // NZ
    return pl.pallas_call(
        weight_kernel,
        out_shape=[
            jax.ShapeDtypeStruct((rows, inner), F32 if dz == 0 else BF16) for dz in range(NZ)
        ],
        compiler_params=vmem_params(),
        cost_estimate=pl.CostEstimate(
            flops=2 * PLANE * tokens * inner * block,
            bytes_accessed=2 * PLANE * tokens * (inner + block) + 3 * block * inner,
            transcendentals=0,
        ),
        name="weight_terms",
    )(*hiddens, *cots)


def values_kernel(*refs):
    hiddens, weights, outs = refs[:PLANE], refs[PLANE : PLANE + NZ], refs[PLANE + NZ :]
    weight = jnp.concatenate([ref[...] for ref in weights], axis=0)
    for (dy, dc), hidden in zip(OFFSETS, hiddens):
        outs[dc][dy] = jnp.dot(hidden[...], weight, preferred_element_type=F32)


def make_value_terms(hiddens, weights):
    tokens, block = hiddens[0].shape
    inner = weights[0].shape[1]
    return pl.pallas_call(
        values_kernel,
        out_shape=[jax.ShapeDtypeStruct((NY, tokens, inner), F32)] * NC,
        compiler_params=vmem_params(),
        cost_estimate=pl.CostEstimate(
            flops=2 * PLANE * tokens * inner * block,
            bytes_accessed=2 * PLANE * tokens * (2 * inner + block) + 2 * block * inner,
            transcendentals=0,
        ),
        name="value_terms",
    )(*hiddens, *weights)


def input_grad_kernel(place, x_ref, gain_ref, scale_ref, *refs):
    grads, out_ref = refs[:PLANE], refs[PLANE]
    position = (place[0], place[1], place[2])
    width = x_ref.shape[1]
    rows = width // (NZ * PLANE)
    scale = scale_ref[...]
    total = jnp.zeros((x_ref.shape[0], rows), F32)
    for (dy, dc), grad in zip(OFFSETS, grads):
        for dz in range(NZ):
            at = pl.ds(feature_start(position, dz, dy, dc, rows), rows)
            scaled = grad[:, dz * rows : (dz + 1) * rows].astype(F32) * gain_ref[:, at]
            total += scaled * (x_ref[:, at].astype(F32) * scale)
    mean = jnp.sum(total, axis=-1, keepdims=True) * (1.0 / width)
    for (dy, dc), grad in zip(OFFSETS, grads):
        for dz in range(NZ):
            at = pl.ds(feature_start(position, dz, dy, dc, rows), rows)
            scaled = grad[:, dz * rows : (dz + 1) * rows].astype(F32) * gain_ref[:, at]
            normed = x_ref[:, at].astype(F32) * scale
            out_ref[:, at] = scale * (scaled - normed * mean)


def make_input_grad(place, inputs, gain, scale, grads):
    tokens, width = inputs.shape
    step = 32
    block = width // PLANE
    return pl.pallas_call(
        input_grad_kernel,
        grid=(tokens // step,),
        in_specs=[
            pl.BlockSpec(memory_space=pltpu.SMEM),
            pl.BlockSpec((step, width), lambda i: (i, 0)),
            pl.BlockSpec((1, width), lambda i: (0, 0)),
            pl.BlockSpec((step, 1), lambda i: (i, 0)),
        ]
        + [pl.BlockSpec((step, block), lambda i: (i, 0))] * PLANE,
        out_specs=pl.BlockSpec((step, width), lambda i: (i, 0)),
        out_shape=jax.ShapeDtypeStruct((tokens, width), F32),
        compiler_params=vmem_params(),
        cost_estimate=pl.CostEstimate(
            flops=12 * tokens * width, bytes_accessed=8 * tokens * width, transcendentals=0
        ),
        name="input_grad",
    )(place, inputs, gain, scale, *grads)


def outer_step(delta, params, moment):
    groups = lax.axis_size("rep")
    rep = lax.axis_index("rep")
    x, half = rep // 2, rep % 2
    count = params.shape[1]
    parts = []
    for dx in (1, 3, 2):
        piece = lax.dynamic_slice_in_dim(delta, ((x + dx) % NX) * 2 * count, 2 * count, 1)
        parts.append(lax.ppermute(piece, "rep", rep_perm(dx, 0)))
    total = lax.dynamic_slice_in_dim(delta, x * 2 * count, 2 * count, 1)
    for part in parts:
        total = total + part
    other = lax.dynamic_slice_in_dim(total, (1 - half) * count, count, 1)
    mine = lax.dynamic_slice_in_dim(total, half * count, count, 1)
    average = (mine + lax.ppermute(other, "rep", rep_perm(0, 1))) / groups
    new_moment = 0.9 * moment + average
    new_params = params - 0.7 * (average + 0.9 * new_moment)
    return new_params, new_moment


def shards(inputs, cotangent, value_weight, norm_gain, outer_delta, outer_params, outer_moment):
    index = lax.axis_index("fsdp")
    z, y, c = split_index(index)
    place = jnp.stack([z, y, c]).astype(jnp.int32)
    gain = norm_gain.reshape(1, -1)
    rows = value_weight.shape[0]

    same = [cotangent] + [send(cotangent, dy=dy) for dy in (1, 2, 3)]
    weights = [value_weight] + [send(value_weight, dz=-dz) for dz in (1, 2, 3)]
    swapped = send(jnp.stack(same), dc=1)
    cots = []
    for dy in range(NY):
        cots += [same[dy], swapped[dy]]

    scale, *mine = make_hidden(place, inputs, gain)
    own_blocks = dict(zip(OFFSETS, mine))
    got = {(0, 0): own_blocks[0, 0]}
    for dy, dc in SENDS:
        got[dy, dc] = send(own_blocks[dy, dc], dy=dy, dc=dc)
    hiddens = [got[offset] for offset in OFFSETS]

    grads = dict(zip(OFFSETS, make_hidden_grad(cots, weights)))
    back = {(0, 0): grads[0, 0]}
    for dy, dc in SENDS:
        back[dy, dc] = send(grads[dy, dc], dy=-dy, dc=dc)
    input_grad = make_input_grad(
        place, inputs, gain, scale, [back[offset] for offset in OFFSETS]
    )

    terms = make_weight_terms(hiddens, cots)
    weight_sum = terms[0]
    for dz in (1, 2, 3):
        weight_sum = weight_sum + send(terms[dz], dz=dz).astype(F32)
    scale_grad = 1.0 / math.sqrt(inputs.shape[0] * lax.axis_size("fsdp"))
    weight_grad = weight_sum * scale_grad
    own_gain = lax.dynamic_slice_in_dim(norm_gain, index * rows, rows, 0)
    gain_grad = jnp.sum(weight_grad * value_weight.astype(F32), axis=1) / own_gain

    keep, give = make_value_terms(hiddens, weights)
    pair = keep + send(give, dc=1)
    values = pair[0]
    for dy in (1, 2, 3):
        values = values + send(pair[dy].astype(BF16), dy=-dy).astype(F32)

    new_params, new_moment = outer_step(outer_delta, outer_params, outer_moment)
    return values, input_grad, weight_grad, gain_grad, new_params, new_moment


def solution(mesh):
    rows = P(("rep", "fsdp"), None)
    in_specs = (rows, rows, rows, P("rep"), rows, P("fsdp", "rep"), P("fsdp", "rep"))
    out_specs = (rows, rows, rows, P(("rep", "fsdp")), P("fsdp", "rep"), P("fsdp", "rep"))
    return jax.shard_map(shards, mesh=mesh, in_specs=in_specs, out_specs=out_specs, check_vma=False)
```

```python
import math

import jax
import jax.numpy as jnp
from jax import lax
from jax.experimental import pallas as pl
from jax.experimental.pallas import tpu as pltpu
from jax.sharding import PartitionSpec as P

F32 = jnp.float32
BF16 = jnp.bfloat16

NZ, NY, NC = 4, 4, 2
PLANE = NY * NC
HALVES = (0, 2, 1, 3)


def place():
    index = lax.axis_index("fsdp")
    return index // PLANE, (index // NC) % NY, index % NC


def swap(array, axis, bits):
    size = lax.axis_size(axis)
    return lax.ppermute(array, axis, [(source, source ^ bits) for source in range(size)])


def exchange_plane(array):
    planes = [[z * PLANE + m for m in range(PLANE)] for z in range(NZ)]
    return lax.all_to_all(array, "fsdp", 0, 0, axis_index_groups=planes)


def after(value, *others):
    return lax.optimization_barrier((value, *others))[0]


def cost(flops, bytes_accessed):
    return pl.CostEstimate(flops=flops, bytes_accessed=bytes_accessed, transcendentals=0)


def feature_start(member, dz, rows):
    return pl.multiple_of((member + (place()[0] ^ dz) * PLANE) * rows, rows)


def norm_kernel(x_ref, gain_ref, scale_ref, out_ref):
    floats = x_ref[...].astype(F32)
    mean = jnp.mean(floats * floats, axis=-1, keepdims=True)
    scale = lax.rsqrt(mean + 1e-05)
    scale_ref[...] = scale
    rows = x_ref.shape[1] // (NZ * PLANE)
    for dz in range(NZ):
        for member in range(PLANE):
            at = pl.ds(feature_start(member, dz, rows), rows)
            normed = x_ref[:, at].astype(F32) * scale
            out_ref[member, :, dz * rows : (dz + 1) * rows] = (normed * gain_ref[:, at]).astype(
                BF16
            )


def make_hidden(inputs, gain):
    tokens, width = inputs.shape
    step = 32
    block = width // PLANE
    return pl.pallas_call(
        norm_kernel,
        grid=(tokens // step,),
        in_specs=[
            pl.BlockSpec((step, width), lambda i: (i, 0)),
            pl.BlockSpec((1, width), lambda i: (0, 0)),
        ],
        out_specs=[
            pl.BlockSpec((step, 1), lambda i: (i, 0)),
            pl.BlockSpec((PLANE, step, block), lambda i: (0, i, 0)),
        ],
        out_shape=[
            jax.ShapeDtypeStruct((tokens, 1), F32),
            jax.ShapeDtypeStruct((PLANE, tokens, block), BF16),
        ],
        cost_estimate=cost(6 * tokens * width, 4 * tokens * width),
        name="norm",
    )(inputs, gain)


def fill_plane(cot_ref, same_ref, other_ref):
    _, y, c = place()
    tokens = cot_ref.shape[0] // PLANE
    for member in range(PLANE):
        dy = y ^ (member // NC)
        first = pl.multiple_of(((dy // 2) + (dy % 2) * 2) * tokens, tokens)
        at = pl.ds(first, tokens)
        cot_ref[member * tokens : (member + 1) * tokens] = jnp.where(
            member % NC == c, same_ref[at], other_ref[at]
        )


def hidden_grad_kernel(same_ref, other_ref, first_ref, second_ref, out_ref, cot_ref):
    step = pl.program_id(0)
    rows = out_ref.shape[2]

    @pl.when(step == 0)
    def _():
        fill_plane(cot_ref, same_ref, other_ref)

    for dz in range(NZ):
        ref, at = ((first_ref, dz // 2), (second_ref, dz // 2))[dz % 2]

        @pl.when(step == dz)
        def _():
            out_ref[...] = (
                lax.dot_general(
                    cot_ref[...],
                    ref[at * rows : (at + 1) * rows],
                    (((1,), (1,)), ((), ())),
                    preferred_element_type=F32,
                )
                .astype(BF16)
                .reshape(out_ref.shape)
            )


def make_hidden_grad(same, other, first, second):
    tokens, inner = same.shape[0] // NY, same.shape[1]
    rows = first.shape[0] // 2
    cots = pl.BlockSpec((NY * tokens, inner), lambda i: (0, 0))
    weight = pl.BlockSpec((2 * rows, inner), lambda i: (0, 0))
    return pl.pallas_call(
        hidden_grad_kernel,
        grid=(NZ,),
        in_specs=[cots, cots, weight, weight],
        out_specs=pl.BlockSpec((PLANE, tokens, rows), lambda i: (0, 0, i)),
        out_shape=jax.ShapeDtypeStruct((PLANE, tokens, NZ * rows), BF16),
        scratch_shapes=[pltpu.VMEM((PLANE * tokens, inner), BF16)],
        cost_estimate=cost(
            2 * PLANE * tokens * inner * NZ * rows,
            2 * PLANE * tokens * (inner + NZ * rows) + 2 * NZ * rows * inner,
        ),
        name="hidden_grad",
    )(same, other, first, second)


def terms_kernel(same_ref, other_ref, first_ref, second_ref, *refs):
    hiddens, (weight_keep, weight_give, keep, give, cot_ref, hidden_ref) = refs[:PLANE], refs[PLANE:]
    _, y, c = place()
    tokens = cot_ref.shape[0] // PLANE
    rows = weight_keep.shape[1]
    fill_plane(cot_ref, same_ref, other_ref)
    for member, hidden in enumerate(hiddens):
        hidden_ref[member * tokens : (member + 1) * tokens] = hidden[0]
    for dz in (1, 3, 0, 2):
        out = weight_give if dz % 2 else weight_keep
        out[dz // 2] = lax.dot_general(
            hidden_ref[:, dz * rows : (dz + 1) * rows],
            cot_ref[...],
            (((0,), (0,)), ((), ())),
            preferred_element_type=F32,
        ).astype(out.dtype)
    first, second = first_ref[...], second_ref[...]
    weight = jnp.concatenate([first[:rows], second[:rows], first[rows:], second[rows:]], axis=0)
    for at, dy in enumerate(HALVES):
        for dc, out in enumerate((keep, give)):
            start = pl.multiple_of(((y ^ dy) * NC + (c ^ dc)) * tokens, tokens)
            out[at] = jnp.dot(
                hidden_ref[pl.ds(start, tokens)], weight, preferred_element_type=F32
            )


def make_terms(same, other, first, second, hidden):
    _, tokens, block = hidden.shape
    inner, rows = first.shape[1], first.shape[0] // 2
    members = [
        pl.BlockSpec((1, tokens, block), lambda i, member=member: (member, 0, 0))
        for member in range(PLANE)
    ]
    cots = pl.BlockSpec((NY * tokens, inner), lambda i: (0, 0))
    weight = pl.BlockSpec((2 * rows, inner), lambda i: (0, 0))
    weight_out = pl.BlockSpec((2, rows, inner), lambda i: (0, 0, 0))
    value_out = pl.BlockSpec((NY, tokens, inner), lambda i: (0, 0, 0))
    return pl.pallas_call(
        terms_kernel,
        grid=(1,),
        in_specs=[cots, cots, weight, weight] + members,
        out_specs=[weight_out] * 2 + [value_out] * 2,
        out_shape=[
            jax.ShapeDtypeStruct((2, rows, inner), F32),
            jax.ShapeDtypeStruct((2, rows, inner), BF16),
            jax.ShapeDtypeStruct((NY, tokens, inner), F32),
            jax.ShapeDtypeStruct((NY, tokens, inner), F32),
        ],
        scratch_shapes=[
            pltpu.VMEM((PLANE * tokens, inner), BF16),
            pltpu.VMEM((PLANE * tokens, block), BF16),
        ],
        cost_estimate=cost(
            4 * PLANE * tokens * inner * block,
            2 * PLANE * tokens * (3 * inner + block) + 2 * block * inner,
        ),
        name="weight_and_value_terms",
    )(same, other, first, second, *[hidden] * PLANE)


def input_grad_kernel(x_ref, gain_ref, scale_ref, grad_ref, out_ref):
    width = x_ref.shape[1]
    rows = width // (NZ * PLANE)
    scale = scale_ref[...]
    total = jnp.zeros((x_ref.shape[0], rows), F32)
    for dz in range(NZ):
        for member in range(PLANE):
            at = pl.ds(feature_start(member, dz, rows), rows)
            grad = grad_ref[member, :, dz * rows : (dz + 1) * rows].astype(F32)
            total += (grad * gain_ref[:, at]) * (x_ref[:, at].astype(F32) * scale)
    mean = jnp.sum(total, axis=-1, keepdims=True) * (1.0 / width)
    for dz in range(NZ):
        for member in range(PLANE):
            at = pl.ds(feature_start(member, dz, rows), rows)
            grad = grad_ref[member, :, dz * rows : (dz + 1) * rows].astype(F32)
            normed = x_ref[:, at].astype(F32) * scale
            out_ref[:, at] = scale * (grad * gain_ref[:, at] - normed * mean)


def make_input_grad(inputs, gain, scale, grads):
    tokens, width = inputs.shape
    step = 32
    block = width // PLANE
    return pl.pallas_call(
        input_grad_kernel,
        grid=(tokens // step,),
        in_specs=[
            pl.BlockSpec((step, width), lambda i: (i, 0)),
            pl.BlockSpec((1, width), lambda i: (0, 0)),
            pl.BlockSpec((step, 1), lambda i: (i, 0)),
            pl.BlockSpec((PLANE, step, block), lambda i: (0, i, 0)),
        ],
        out_specs=pl.BlockSpec((step, width), lambda i: (i, 0)),
        out_shape=jax.ShapeDtypeStruct((tokens, width), F32),
        cost_estimate=cost(12 * tokens * width, 8 * tokens * width),
        name="input_grad",
    )(inputs, gain, scale, grads)


def halve_columns(total, bits):
    half = total.shape[1] // 2
    mine = lax.axis_index("rep") // bits % 2
    give = lax.dynamic_slice_in_dim(total, (1 - mine) * half, half, 1)
    keep = lax.dynamic_slice_in_dim(total, mine * half, half, 1)
    return keep + swap(give, "rep", bits)


def outer_step(total, params, moment):
    average = total / lax.axis_size("rep")
    new_moment = 0.9 * moment + average
    new_params = params - 0.7 * (average + 0.9 * new_moment)
    return new_params, new_moment


def gather_pairs(array, bits):
    array = jnp.concatenate([array, swap(array, "fsdp", 2 * bits)], axis=0)
    return array, swap(array, "fsdp", bits)


def shards(inputs, cotangent, value_weight, norm_gain, outer_delta, outer_params, outer_moment):
    index = lax.axis_index("fsdp")
    gain = norm_gain.reshape(1, -1)
    rows = value_weight.shape[0]

    same = jnp.concatenate(gather_pairs(cotangent, NC), axis=0)
    other = swap(same, "fsdp", 1)
    first, second = gather_pairs(value_weight, PLANE)
    delta = halve_columns(outer_delta, 4)

    scale, blocks = make_hidden(inputs, gain)
    hidden = exchange_plane(after(blocks, same, first))

    delta = halve_columns(halve_columns(delta, 2), 1)
    new_params, new_moment = outer_step(delta, outer_params, outer_moment)

    grads = make_hidden_grad(after(same, same), other, first, second)
    back = exchange_plane(grads)

    weight_keep, weight_give, keep, give = make_terms(
        same, after(other, grads), first, second, hidden
    )
    weight_sums = weight_keep + swap(weight_give, "fsdp", PLANE).astype(F32)
    weight_sum = weight_sums[0] + swap(weight_sums[1].astype(BF16), "fsdp", 2 * PLANE).astype(F32)
    scale_grad = 1.0 / math.sqrt(inputs.shape[0] * lax.axis_size("fsdp"))
    weight_grad = weight_sum * scale_grad
    own_gain = lax.dynamic_slice_in_dim(norm_gain, index * rows, rows, 0)
    gain_grad = jnp.sum(weight_grad * value_weight.astype(F32), axis=1) / own_gain

    pair = keep + swap(give, "fsdp", 1)
    pair = pair[:2] + swap(pair[2:].astype(BF16), "fsdp", NC).astype(F32)
    values = pair[0] + swap(pair[1].astype(BF16), "fsdp", 2 * NC).astype(F32)
    input_grad = make_input_grad(inputs, gain, scale, after(back, weight_sums, pair))
    return values, input_grad, weight_grad, gain_grad, new_params, new_moment


def solution(mesh):
    rows = P(("rep", "fsdp"), None)
    in_specs = (rows, rows, rows, P("rep"), rows, P("fsdp", "rep"), P("fsdp", "rep"))
    out_specs = (rows, rows, rows, P(("rep", "fsdp")), P("fsdp", "rep"), P("fsdp", "rep"))
    return jax.shard_map(shards, mesh=mesh, in_specs=in_specs, out_specs=out_specs, check_vma=False)
```

```python
import math

import jax
import jax.numpy as jnp
from jax import lax
from jax.experimental import pallas as pl
from jax.experimental.pallas import tpu as pltpu
from jax.sharding import PartitionSpec as P

F32 = jnp.float32
BF16 = jnp.bfloat16

NZ, NY, NC = 4, 4, 2
PLANE = NY * NC
HALVES = (0, 2, 1, 3)


def place():
    index = lax.axis_index("fsdp")
    return index // PLANE, (index // NC) % NY, index % NC


def swap(array, axis, bits):
    size = lax.axis_size(axis)
    return lax.ppermute(array, axis, [(source, source ^ bits) for source in range(size)])


def exchange_plane(array):
    planes = [[z * PLANE + m for m in range(PLANE)] for z in range(NZ)]
    return lax.all_to_all(array, "fsdp", 0, 0, axis_index_groups=planes)


def together(*values):
    return lax.optimization_barrier(values)


def cost(flops, bytes_accessed):
    return pl.CostEstimate(flops=flops, bytes_accessed=bytes_accessed, transcendentals=0)


def roomy():
    return pltpu.CompilerParams(vmem_limit_bytes=62 * 2**20)


def feature_start(member, dz, rows):
    return pl.multiple_of((member + (place()[0] ^ dz) * PLANE) * rows, rows)


def norm_kernel(x_ref, gain_ref, scale_ref, out_ref):
    floats = x_ref[...].astype(F32)
    mean = jnp.mean(floats * floats, axis=-1, keepdims=True)
    scale = lax.rsqrt(mean + 1e-05)
    scale_ref[...] = scale
    rows = x_ref.shape[1] // (NZ * PLANE)
    for dz in range(NZ):
        for member in range(PLANE):
            at = pl.ds(feature_start(member, dz, rows), rows)
            normed = x_ref[:, at].astype(F32) * scale
            out_ref[member, :, dz * rows : (dz + 1) * rows] = (normed * gain_ref[:, at]).astype(
                BF16
            )


def make_hidden(inputs, gain):
    tokens, width = inputs.shape
    step = 32
    block = width // PLANE
    return pl.pallas_call(
        norm_kernel,
        grid=(tokens // step,),
        in_specs=[
            pl.BlockSpec((step, width), lambda i: (i, 0)),
            pl.BlockSpec((1, width), lambda i: (0, 0)),
        ],
        out_specs=[
            pl.BlockSpec((step, 1), lambda i: (i, 0)),
            pl.BlockSpec((PLANE, step, block), lambda i: (0, i, 0)),
        ],
        out_shape=[
            jax.ShapeDtypeStruct((tokens, 1), F32),
            jax.ShapeDtypeStruct((PLANE, tokens, block), BF16),
        ],
        cost_estimate=cost(6 * tokens * width, 4 * tokens * width),
        name="norm",
    )(inputs, gain)


def fill_plane(cot_ref, same_ref, other_ref):
    _, y, c = place()
    tokens = cot_ref.shape[0] // PLANE
    for member in range(PLANE):
        dy = y ^ (member // NC)
        first = pl.multiple_of(((dy // 2) + (dy % 2) * 2) * tokens, tokens)
        at = pl.ds(first, tokens)
        cot_ref[member * tokens : (member + 1) * tokens] = jnp.where(
            member % NC == c, same_ref[at], other_ref[at]
        )


def hidden_grad_kernel(same_ref, other_ref, first_ref, second_ref, out_ref, cot_ref):
    step = pl.program_id(0)
    rows = out_ref.shape[2]

    @pl.when(step == 0)
    def _():
        fill_plane(cot_ref, same_ref, other_ref)

    for dz in range(NZ):
        ref, at = ((first_ref, dz // 2), (second_ref, dz // 2))[dz % 2]

        @pl.when(step == dz)
        def _():
            out_ref[...] = (
                lax.dot_general(
                    cot_ref[...],
                    ref[at * rows : (at + 1) * rows],
                    (((1,), (1,)), ((), ())),
                    preferred_element_type=F32,
                )
                .astype(BF16)
                .reshape(out_ref.shape)
            )


def make_hidden_grad(same, other, first, second):
    tokens, inner = same.shape[0] // NY, same.shape[1]
    rows = first.shape[0] // 2
    cots = pl.BlockSpec((NY * tokens, inner), lambda i: (0, 0))
    weight = pl.BlockSpec((2 * rows, inner), lambda i: (0, 0))
    return pl.pallas_call(
        hidden_grad_kernel,
        grid=(NZ,),
        in_specs=[cots, cots, weight, weight],
        out_specs=pl.BlockSpec((PLANE, tokens, rows), lambda i: (0, 0, i)),
        out_shape=jax.ShapeDtypeStruct((PLANE, tokens, NZ * rows), BF16),
        scratch_shapes=[pltpu.VMEM((PLANE * tokens, inner), BF16)],
        cost_estimate=cost(
            2 * PLANE * tokens * inner * NZ * rows,
            2 * PLANE * tokens * (inner + NZ * rows) + 2 * NZ * rows * inner,
        ),
        name="hidden_grad",
    )(same, other, first, second)


def terms_kernel(same_ref, other_ref, first_ref, second_ref, *refs):
    hiddens, (*outs, keep, give, cot_ref, hidden_ref) = refs[:PLANE], refs[PLANE:]
    _, y, c = place()
    tokens = cot_ref.shape[0] // PLANE
    rows = outs[0].shape[0]
    fill_plane(cot_ref, same_ref, other_ref)
    for member, hidden in enumerate(hiddens):
        hidden_ref[member * tokens : (member + 1) * tokens] = hidden[0]
    for dz, out in enumerate(outs):
        out[...] = lax.dot_general(
            hidden_ref[:, dz * rows : (dz + 1) * rows],
            cot_ref[...],
            (((0,), (0,)), ((), ())),
            preferred_element_type=F32,
        ).astype(out.dtype)
    first, second = first_ref[...], second_ref[...]
    weight = jnp.concatenate([first[:rows], second[:rows], first[rows:], second[rows:]], axis=0)
    for at, dy in enumerate(HALVES):
        for dc, out in enumerate((keep, give)):
            start = pl.multiple_of(((y ^ dy) * NC + (c ^ dc)) * tokens, tokens)
            out[at] = jnp.dot(
                hidden_ref[pl.ds(start, tokens)], weight, preferred_element_type=F32
            )


def make_terms(same, other, first, second, hidden):
    _, tokens, block = hidden.shape
    inner, rows = same.shape[1], block // NZ
    members = [
        pl.BlockSpec((1, tokens, block), lambda i, member=member: (member, 0, 0))
        for member in range(PLANE)
    ]
    cots = pl.BlockSpec((NY * tokens, inner), lambda i: (0, 0))
    weight = pl.BlockSpec((2 * rows, inner), lambda i: (0, 0))
    return pl.pallas_call(
        terms_kernel,
        grid=(1,),
        in_specs=[cots, cots, weight, weight] + members,
        out_specs=[pl.BlockSpec((rows, inner), lambda i: (0, 0))] * NZ
        + [pl.BlockSpec((NY, tokens, inner), lambda i: (0, 0, 0))] * NC,
        out_shape=[
            jax.ShapeDtypeStruct((rows, inner), BF16 if dz else F32) for dz in range(NZ)
        ]
        + [jax.ShapeDtypeStruct((NY, tokens, inner), F32)] * NC,
        scratch_shapes=[
            pltpu.VMEM((PLANE * tokens, inner), BF16),
            pltpu.VMEM((PLANE * tokens, block), BF16),
        ],
        compiler_params=roomy(),
        cost_estimate=cost(
            4 * PLANE * tokens * inner * block,
            2 * PLANE * tokens * (3 * inner + block) + 2 * block * inner,
        ),
        name="weight_and_value_terms",
    )(same, other, first, second, *[hidden] * PLANE)


def input_grad_kernel(x_ref, gain_ref, scale_ref, grad_ref, out_ref):
    width = x_ref.shape[1]
    rows = width // (NZ * PLANE)
    scale = scale_ref[...]
    total = jnp.zeros((x_ref.shape[0], rows), F32)
    for dz in range(NZ):
        for member in range(PLANE):
            at = pl.ds(feature_start(member, dz, rows), rows)
            grad = grad_ref[member, :, dz * rows : (dz + 1) * rows].astype(F32)
            total += (grad * gain_ref[:, at]) * (x_ref[:, at].astype(F32) * scale)
    mean = jnp.sum(total, axis=-1, keepdims=True) * (1.0 / width)
    for dz in range(NZ):
        for member in range(PLANE):
            at = pl.ds(feature_start(member, dz, rows), rows)
            grad = grad_ref[member, :, dz * rows : (dz + 1) * rows].astype(F32)
            normed = x_ref[:, at].astype(F32) * scale
            out_ref[:, at] = scale * (grad * gain_ref[:, at] - normed * mean)


def make_input_grad(inputs, gain, scale, grads):
    tokens, width = inputs.shape
    step = 32
    block = width // PLANE
    return pl.pallas_call(
        input_grad_kernel,
        grid=(tokens // step,),
        in_specs=[
            pl.BlockSpec((step, width), lambda i: (i, 0)),
            pl.BlockSpec((1, width), lambda i: (0, 0)),
            pl.BlockSpec((step, 1), lambda i: (i, 0)),
            pl.BlockSpec((PLANE, step, block), lambda i: (0, i, 0)),
        ],
        out_specs=pl.BlockSpec((step, width), lambda i: (i, 0)),
        out_shape=jax.ShapeDtypeStruct((tokens, width), F32),
        compiler_params=roomy(),
        cost_estimate=cost(12 * tokens * width, 8 * tokens * width),
        name="input_grad",
    )(inputs, gain, scale, grads)


def sum_over_x(delta):
    width = delta.shape[1] // 4
    x = lax.axis_index("rep") // 2
    total = lax.dynamic_slice_in_dim(delta, x * width, width, 1)
    for dx in (2, 1, 3):
        piece = lax.dynamic_slice_in_dim(delta, (x ^ dx) * width, width, 1)
        total = total + swap(piece.astype(BF16), "rep", 2 * dx).astype(F32)
    return total


def sum_over_halves(delta):
    width = delta.shape[1] // 2
    half = lax.axis_index("rep") % 2
    give = lax.dynamic_slice_in_dim(delta, (1 - half) * width, width, 1)
    return lax.dynamic_slice_in_dim(delta, half * width, width, 1) + swap(give, "rep", 1)


def outer_step(total, params, moment):
    average = total / lax.axis_size("rep")
    new_moment = 0.9 * moment + average
    new_params = params - 0.7 * (average + 0.9 * new_moment)
    return new_params, new_moment


def gather_pairs(array, bits):
    array = jnp.concatenate([array, swap(array, "fsdp", 2 * bits)], axis=0)
    return array, swap(array, "fsdp", bits)


def shards(inputs, cotangent, value_weight, norm_gain, outer_delta, outer_params, outer_moment):
    index = lax.axis_index("fsdp")
    gain = norm_gain.reshape(1, -1)
    rows = value_weight.shape[0]

    first = jnp.concatenate([value_weight, swap(value_weight, "fsdp", 2 * PLANE)], axis=0)
    same = jnp.concatenate(gather_pairs(cotangent, NC), axis=0)
    scale, blocks = make_hidden(inputs, gain)
    blocks, same, first = together(blocks, same, first)

    hidden = exchange_plane(blocks)
    second = swap(first, "fsdp", PLANE)
    other = swap(same, "fsdp", 1)
    delta = sum_over_x(outer_delta)
    same, delta = together(same, delta)
    delta = sum_over_halves(delta)
    new_params, new_moment = outer_step(delta, outer_params, outer_moment)
    grads = make_hidden_grad(same, other, first, second)
    hidden, new_moment = together(hidden, new_moment)
    back = exchange_plane(grads)

    *terms, keep, give = make_terms(same, other, first, second, hidden)
    got = [swap(terms[dz], "fsdp", dz * PLANE) for dz in (1, 2, 3)]
    (pair,) = together(keep + swap(give, "fsdp", 1))
    back, own = together(back, pair[0])
    near = swap(pair[2:].astype(BF16), "fsdp", NC)
    input_grad = make_input_grad(inputs, gain, scale, back)
    input_grad, near, *got = together(input_grad, near, *got)
    near = near.astype(F32)
    far = swap((pair[1] + near[1]).astype(BF16), "fsdp", 2 * NC).astype(F32)
    values = own + near[0] + far
    weight_sum = terms[0]
    for part in got:
        weight_sum = weight_sum + part.astype(F32)
    scale_grad = 1.0 / math.sqrt(inputs.shape[0] * lax.axis_size("fsdp"))
    weight_grad = weight_sum * scale_grad
    own_gain = lax.dynamic_slice_in_dim(norm_gain, index * rows, rows, 0)
    gain_grad = jnp.sum(weight_grad * value_weight.astype(F32), axis=1) / own_gain
    return values, input_grad, weight_grad, gain_grad, new_params, new_moment


def solution(mesh):
    rows = P(("rep", "fsdp"), None)
    in_specs = (rows, rows, rows, P("rep"), rows, P("fsdp", "rep"), P("fsdp", "rep"))
    out_specs = (rows, rows, rows, P(("rep", "fsdp")), P("fsdp", "rep"), P("fsdp", "rep"))
    return jax.shard_map(shards, mesh=mesh, in_specs=in_specs, out_specs=out_specs, check_vma=False)
```

```python
import math

import jax
import jax.numpy as jnp
from jax import lax
from jax.experimental import pallas as pl
from jax.experimental.pallas import tpu as pltpu
from jax.sharding import PartitionSpec as P

F32 = jnp.float32
BF16 = jnp.bfloat16

NZ, NY, NC = 4, 4, 2
PLANE = NY * NC
HALVES = (0, 2, 1, 3)


def place():
    index = lax.axis_index("fsdp")
    return index // PLANE, (index // NC) % NY, index % NC


def swap(array, axis, bits):
    size = lax.axis_size(axis)
    return lax.ppermute(array, axis, [(source, source ^ bits) for source in range(size)])


def exchange_plane(array):
    planes = [[z * PLANE + m for m in range(PLANE)] for z in range(NZ)]
    return lax.all_to_all(array, "fsdp", 0, 0, axis_index_groups=planes)


def together(*values):
    return lax.optimization_barrier(values)


def cost(flops, bytes_accessed):
    return pl.CostEstimate(flops=flops, bytes_accessed=bytes_accessed, transcendentals=0)


def roomy():
    return pltpu.CompilerParams(vmem_limit_bytes=62 * 2**20)


def feature_start(member, dz, rows):
    return pl.multiple_of((member + (place()[0] ^ dz) * PLANE) * rows, rows)


def norm_kernel(x_ref, gain_ref, scale_ref, out_ref):
    floats = x_ref[...].astype(F32)
    mean = jnp.mean(floats * floats, axis=-1, keepdims=True)
    scale = lax.rsqrt(mean + 1e-05)
    scale_ref[...] = scale
    rows = x_ref.shape[1] // (NZ * PLANE)
    for dz in range(NZ):
        for member in range(PLANE):
            at = pl.ds(feature_start(member, dz, rows), rows)
            normed = x_ref[:, at].astype(F32) * scale
            out_ref[member, :, dz * rows : (dz + 1) * rows] = (normed * gain_ref[:, at]).astype(
                BF16
            )


def make_hidden(inputs, gain):
    tokens, width = inputs.shape
    step = 32
    block = width // PLANE
    return pl.pallas_call(
        norm_kernel,
        grid=(tokens // step,),
        in_specs=[
            pl.BlockSpec((step, width), lambda i: (i, 0)),
            pl.BlockSpec((1, width), lambda i: (0, 0)),
        ],
        out_specs=[
            pl.BlockSpec((step, 1), lambda i: (i, 0)),
            pl.BlockSpec((PLANE, step, block), lambda i: (0, i, 0)),
        ],
        out_shape=[
            jax.ShapeDtypeStruct((tokens, 1), F32),
            jax.ShapeDtypeStruct((PLANE, tokens, block), BF16),
        ],
        cost_estimate=cost(6 * tokens * width, 4 * tokens * width),
        name="norm",
    )(inputs, gain)


def fill_plane(cot_ref, same_ref, other_ref):
    _, y, c = place()
    tokens = cot_ref.shape[0] // PLANE
    for member in range(PLANE):
        dy = y ^ (member // NC)
        first = pl.multiple_of(((dy // 2) + (dy % 2) * 2) * tokens, tokens)
        at = pl.ds(first, tokens)
        cot_ref[member * tokens : (member + 1) * tokens] = jnp.where(
            member % NC == c, same_ref[at], other_ref[at]
        )


def hidden_grad_kernel(same_ref, other_ref, first_ref, second_ref, out_ref, cot_ref):
    step = pl.program_id(0)
    rows = out_ref.shape[2]

    @pl.when(step == 0)
    def _():
        fill_plane(cot_ref, same_ref, other_ref)

    for dz in range(NZ):
        ref, at = ((first_ref, dz // 2), (second_ref, dz // 2))[dz % 2]

        @pl.when(step == dz)
        def _():
            out_ref[...] = (
                lax.dot_general(
                    cot_ref[...],
                    ref[at * rows : (at + 1) * rows],
                    (((1,), (1,)), ((), ())),
                    preferred_element_type=F32,
                )
                .astype(BF16)
                .reshape(out_ref.shape)
            )


def make_hidden_grad(same, other, first, second):
    tokens, inner = same.shape[0] // NY, same.shape[1]
    rows = first.shape[0] // 2
    cots = pl.BlockSpec((NY * tokens, inner), lambda i: (0, 0))
    weight = pl.BlockSpec((2 * rows, inner), lambda i: (0, 0))
    return pl.pallas_call(
        hidden_grad_kernel,
        grid=(NZ,),
        in_specs=[cots, cots, weight, weight],
        out_specs=pl.BlockSpec((PLANE, tokens, rows), lambda i: (0, 0, i)),
        out_shape=jax.ShapeDtypeStruct((PLANE, tokens, NZ * rows), BF16),
        scratch_shapes=[pltpu.VMEM((PLANE * tokens, inner), BF16)],
        cost_estimate=cost(
            2 * PLANE * tokens * inner * NZ * rows,
            2 * PLANE * tokens * (inner + NZ * rows) + 2 * NZ * rows * inner,
        ),
        name="hidden_grad",
    )(same, other, first, second)


def terms_kernel(same_ref, other_ref, first_ref, second_ref, *refs):
    hiddens, (*outs, keep, give, cot_ref, hidden_ref) = refs[:PLANE], refs[PLANE:]
    _, y, c = place()
    tokens = cot_ref.shape[0] // PLANE
    rows = outs[0].shape[0]
    fill_plane(cot_ref, same_ref, other_ref)
    for member, hidden in enumerate(hiddens):
        hidden_ref[member * tokens : (member + 1) * tokens] = hidden[0]
    for dz, out in enumerate(outs):
        out[...] = lax.dot_general(
            hidden_ref[:, dz * rows : (dz + 1) * rows],
            cot_ref[...],
            (((0,), (0,)), ((), ())),
            preferred_element_type=F32,
        ).astype(out.dtype)
    first, second = first_ref[...], second_ref[...]
    weight = jnp.concatenate([first[:rows], second[:rows], first[rows:], second[rows:]], axis=0)
    for dy in range(NY):
        for dc, out in enumerate((keep, give)):
            start = pl.multiple_of(((y ^ dy) * NC + (c ^ dc)) * tokens, tokens)
            out[dy] = jnp.dot(
                hidden_ref[pl.ds(start, tokens)], weight, preferred_element_type=F32
            )


def make_terms(same, other, first, second, hidden):
    _, tokens, block = hidden.shape
    inner, rows = same.shape[1], block // NZ
    members = [
        pl.BlockSpec((1, tokens, block), lambda i, member=member: (member, 0, 0))
        for member in range(PLANE)
    ]
    cots = pl.BlockSpec((NY * tokens, inner), lambda i: (0, 0))
    weight = pl.BlockSpec((2 * rows, inner), lambda i: (0, 0))
    return pl.pallas_call(
        terms_kernel,
        grid=(1,),
        in_specs=[cots, cots, weight, weight] + members,
        out_specs=[pl.BlockSpec((rows, inner), lambda i: (0, 0))] * NZ
        + [pl.BlockSpec((NY, tokens, inner), lambda i: (0, 0, 0))] * NC,
        out_shape=[
            jax.ShapeDtypeStruct((rows, inner), BF16 if dz else F32) for dz in range(NZ)
        ]
        + [jax.ShapeDtypeStruct((NY, tokens, inner), F32)] * NC,
        scratch_shapes=[
            pltpu.VMEM((PLANE * tokens, inner), BF16),
            pltpu.VMEM((PLANE * tokens, block), BF16),
        ],
        compiler_params=roomy(),
        cost_estimate=cost(
            4 * PLANE * tokens * inner * block,
            2 * PLANE * tokens * (3 * inner + block) + 2 * block * inner,
        ),
        name="weight_and_value_terms",
    )(same, other, first, second, *[hidden] * PLANE)


def input_grad_kernel(x_ref, gain_ref, scale_ref, *refs):
    grads, out_ref = refs[:NY], refs[NY]
    width = x_ref.shape[1]
    rows = width // (NZ * PLANE)
    scale = scale_ref[...]
    total = jnp.zeros((x_ref.shape[0], rows), F32)
    for dz in range(NZ):
        for member in range(PLANE):
            at = pl.ds(feature_start(member, dz, rows), rows)
            grad = grads[member // NC][member % NC, :, dz * rows : (dz + 1) * rows]
            scaled = grad.astype(F32) * gain_ref[:, at]
            out_ref[:, at] = scaled
            total += scaled * x_ref[:, at].astype(F32)
    mean = scale * jnp.sum(total, axis=-1, keepdims=True) * (1.0 / width)
    factor = scale * scale * mean
    for block in range(NZ * PLANE):
        at = slice(block * rows, (block + 1) * rows)
        out_ref[:, at] = scale * out_ref[:, at] - x_ref[:, at].astype(F32) * factor


def make_input_grad(inputs, gain, scale, grads):
    tokens, width = inputs.shape
    step = 32
    block = width // PLANE
    members = [
        pl.BlockSpec((NC, step, block), lambda i, pair=pair: (pair, i, 0)) for pair in range(NY)
    ]
    return pl.pallas_call(
        input_grad_kernel,
        grid=(tokens // step,),
        in_specs=[
            pl.BlockSpec((step, width), lambda i: (i, 0)),
            pl.BlockSpec((1, width), lambda i: (0, 0)),
            pl.BlockSpec((step, 1), lambda i: (i, 0)),
        ]
        + members,
        out_specs=pl.BlockSpec((step, width), lambda i: (i, 0)),
        out_shape=jax.ShapeDtypeStruct((tokens, width), F32),
        compiler_params=roomy(),
        cost_estimate=cost(9 * tokens * width, 8 * tokens * width),
        name="input_grad",
    )(inputs, gain, scale, *[grads] * NY)


def sum_over_x(delta):
    width = delta.shape[1] // 4
    x = lax.axis_index("rep") // 2
    total = lax.dynamic_slice_in_dim(delta, x * width, width, 1)
    for dx in (2, 1, 3):
        piece = lax.dynamic_slice_in_dim(delta, (x ^ dx) * width, width, 1)
        total = total + swap(piece.astype(BF16), "rep", 2 * dx).astype(F32)
    return total


def sum_over_halves(delta):
    width = delta.shape[1] // 2
    half = lax.axis_index("rep") % 2
    give = lax.dynamic_slice_in_dim(delta, (1 - half) * width, width, 1)
    return lax.dynamic_slice_in_dim(delta, half * width, width, 1) + swap(give, "rep", 1)


def outer_step(total, params, moment):
    average = total / lax.axis_size("rep")
    new_moment = 0.9 * moment + average
    new_params = params - 0.7 * (average + 0.9 * new_moment)
    return new_params, new_moment


def gather_pairs(array, bits):
    array = jnp.concatenate([array, swap(array, "fsdp", 2 * bits)], axis=0)
    return array, swap(array, "fsdp", bits)


def shards(inputs, cotangent, value_weight, norm_gain, outer_delta, outer_params, outer_moment):
    index = lax.axis_index("fsdp")
    gain = norm_gain.reshape(1, -1)
    rows = value_weight.shape[0]

    first = jnp.concatenate([value_weight, swap(value_weight, "fsdp", 2 * PLANE)], axis=0)
    same = jnp.concatenate(
        [cotangent] + [swap(cotangent, "fsdp", dy * NC) for dy in HALVES[1:]], axis=0
    )
    scale, blocks = make_hidden(inputs, gain)
    blocks, same, first = together(blocks, same, first)

    hidden = exchange_plane(blocks)
    second = swap(first, "fsdp", PLANE)
    other = swap(same, "fsdp", 1)
    own_gain = lax.dynamic_slice_in_dim(norm_gain, index * rows, rows, 0)
    weight_by_gain = value_weight.astype(F32) / own_gain[:, None]
    delta = sum_over_x(outer_delta)
    same, delta = together(same, delta)
    delta = sum_over_halves(delta)
    new_params, new_moment = outer_step(delta, outer_params, outer_moment)
    grads = make_hidden_grad(same, other, first, second)
    hidden, new_moment, weight_by_gain = together(hidden, new_moment, weight_by_gain)
    back = exchange_plane(grads)

    *terms, keep, give = make_terms(same, other, first, second, hidden)
    got = [swap(terms[dz], "fsdp", dz * PLANE) for dz in (1, 2, 3)]
    (pair,) = together(keep + swap(give, "fsdp", 1))
    back, own = together(back, pair[0])
    far = swap(pair[2:].astype(BF16), "fsdp", 2 * NC)
    input_grad = make_input_grad(inputs, gain, scale, back)
    input_grad, far, *got = together(input_grad, far, *got)
    far = far.astype(F32)
    near = swap((pair[1] + far[1]).astype(BF16), "fsdp", NC).astype(F32)
    values = own + far[0] + near
    weight_sum = terms[0]
    for part in got:
        weight_sum = weight_sum + part.astype(F32)
    scale_grad = 1.0 / math.sqrt(inputs.shape[0] * lax.axis_size("fsdp"))
    weight_grad = weight_sum * scale_grad
    gain_grad = jnp.sum(weight_grad * weight_by_gain, axis=1)
    return values, input_grad, weight_grad, gain_grad, new_params, new_moment


def solution(mesh):
    rows = P(("rep", "fsdp"), None)
    in_specs = (rows, rows, rows, P("rep"), rows, P("fsdp", "rep"), P("fsdp", "rep"))
    out_specs = (rows, rows, rows, P(("rep", "fsdp")), P("fsdp", "rep"), P("fsdp", "rep"))
    return jax.shard_map(shards, mesh=mesh, in_specs=in_specs, out_specs=out_specs, check_vma=False)
```

```python
import math

import jax
import jax.numpy as jnp
from jax import lax
from jax.experimental import pallas as pl
from jax.experimental.pallas import tpu as pltpu
from jax.sharding import PartitionSpec as P

F32 = jnp.float32
BF16 = jnp.bfloat16

NZ, NY, NC = 4, 4, 2
PLANE = NY * NC
HALVES = (0, 2, 1, 3)


def place():
    index = lax.axis_index("fsdp")
    return index // PLANE, (index // NC) % NY, index % NC


def swap(array, axis, bits):
    size = lax.axis_size(axis)
    return lax.ppermute(array, axis, [(source, source ^ bits) for source in range(size)])


def exchange_plane(array):
    planes = [[z * PLANE + m for m in range(PLANE)] for z in range(NZ)]
    return lax.all_to_all(array, "fsdp", 0, 0, axis_index_groups=planes)


def together(*values):
    return lax.optimization_barrier(values)


def cost(flops, bytes_accessed):
    return pl.CostEstimate(flops=flops, bytes_accessed=bytes_accessed, transcendentals=0)


def roomy(mib=62):
    return pltpu.CompilerParams(vmem_limit_bytes=mib * 2**20)


def feature_start(member, dz, rows):
    return pl.multiple_of((member + (place()[0] ^ dz) * PLANE) * rows, rows)


def norm_kernel(x_ref, gain_ref, scale_ref, out_ref):
    floats = x_ref[...].astype(F32)
    mean = jnp.mean(floats * floats, axis=-1, keepdims=True)
    scale = lax.rsqrt(mean + 1e-05)
    scale_ref[...] = scale
    rows = x_ref.shape[1] // (NZ * PLANE)
    for dz in range(NZ):
        for member in range(PLANE):
            at = pl.ds(feature_start(member, dz, rows), rows)
            normed = x_ref[:, at].astype(F32) * scale
            out_ref[member, :, dz * rows : (dz + 1) * rows] = (normed * gain_ref[:, at]).astype(
                BF16
            )


def make_hidden(inputs, gain):
    tokens, width = inputs.shape
    step = 32
    block = width // PLANE
    return pl.pallas_call(
        norm_kernel,
        grid=(tokens // step,),
        in_specs=[
            pl.BlockSpec((step, width), lambda i: (i, 0)),
            pl.BlockSpec((1, width), lambda i: (0, 0)),
        ],
        out_specs=[
            pl.BlockSpec((step, 1), lambda i: (i, 0)),
            pl.BlockSpec((PLANE, step, block), lambda i: (0, i, 0)),
        ],
        out_shape=[
            jax.ShapeDtypeStruct((tokens, 1), F32),
            jax.ShapeDtypeStruct((PLANE, tokens, block), BF16),
        ],
        cost_estimate=cost(6 * tokens * width, 4 * tokens * width),
        name="norm",
    )(inputs, gain)


def fill_plane(cot_ref, same_ref, other_ref):
    _, y, c = place()
    tokens = cot_ref.shape[0] // PLANE
    for member in range(PLANE):
        dy = y ^ (member // NC)
        first = pl.multiple_of(((dy // 2) + (dy % 2) * 2) * tokens, tokens)
        at = pl.ds(first, tokens)
        cot_ref[member * tokens : (member + 1) * tokens] = jnp.where(
            member % NC == c, same_ref[at], other_ref[at]
        )


def hidden_grad_kernel(same_ref, other_ref, first_ref, second_ref, out_ref, cot_ref):
    step = pl.program_id(0)
    rows = out_ref.shape[2]

    @pl.when(step == 0)
    def _():
        fill_plane(cot_ref, same_ref, other_ref)

    for dz in range(NZ):
        ref, at = ((first_ref, dz // 2), (second_ref, dz // 2))[dz % 2]

        @pl.when(step == dz)
        def _():
            out_ref[...] = (
                lax.dot_general(
                    cot_ref[...],
                    ref[at * rows : (at + 1) * rows],
                    (((1,), (1,)), ((), ())),
                    preferred_element_type=F32,
                )
                .astype(BF16)
                .reshape(out_ref.shape)
            )


def make_hidden_grad(same, other, first, second):
    tokens, inner = same.shape[0] // NY, same.shape[1]
    rows = first.shape[0] // 2
    cots = pl.BlockSpec((NY * tokens, inner), lambda i: (0, 0))
    weight = pl.BlockSpec((2 * rows, inner), lambda i: (0, 0))
    return pl.pallas_call(
        hidden_grad_kernel,
        grid=(NZ,),
        in_specs=[cots, cots, weight, weight],
        out_specs=pl.BlockSpec((PLANE, tokens, rows), lambda i: (0, 0, i)),
        out_shape=jax.ShapeDtypeStruct((PLANE, tokens, NZ * rows), BF16),
        scratch_shapes=[pltpu.VMEM((PLANE * tokens, inner), BF16)],
        cost_estimate=cost(
            2 * PLANE * tokens * inner * NZ * rows,
            2 * PLANE * tokens * (inner + NZ * rows) + 2 * NZ * rows * inner,
        ),
        name="hidden_grad",
    )(same, other, first, second)


def terms_kernel(same_ref, other_ref, first_ref, second_ref, *refs):
    hiddens, (*outs, keep, give, cot_ref, hidden_ref) = refs[:PLANE], refs[PLANE:]
    _, y, c = place()
    tokens = cot_ref.shape[0] // PLANE
    rows = outs[0].shape[0]
    fill_plane(cot_ref, same_ref, other_ref)
    for member, hidden in enumerate(hiddens):
        hidden_ref[member * tokens : (member + 1) * tokens] = hidden[0]
    for dz, out in enumerate(outs):
        out[...] = lax.dot_general(
            hidden_ref[:, dz * rows : (dz + 1) * rows],
            cot_ref[...],
            (((0,), (0,)), ((), ())),
            preferred_element_type=F32,
        ).astype(out.dtype)
    first, second = first_ref[...], second_ref[...]
    weight = jnp.concatenate([first[:rows], second[:rows], first[rows:], second[rows:]], axis=0)
    for dy in range(NY):
        for dc, out in enumerate((keep, give)):
            start = pl.multiple_of(((y ^ dy) * NC + (c ^ dc)) * tokens, tokens)
            out[dy] = jnp.dot(
                hidden_ref[pl.ds(start, tokens)], weight, preferred_element_type=F32
            )


def make_terms(same, other, first, second, hidden):
    _, tokens, block = hidden.shape
    inner, rows = same.shape[1], block // NZ
    members = [
        pl.BlockSpec((1, tokens, block), lambda i, member=member: (member, 0, 0))
        for member in range(PLANE)
    ]
    cots = pl.BlockSpec((NY * tokens, inner), lambda i: (0, 0))
    weight = pl.BlockSpec((2 * rows, inner), lambda i: (0, 0))
    return pl.pallas_call(
        terms_kernel,
        grid=(1,),
        in_specs=[cots, cots, weight, weight] + members,
        out_specs=[pl.BlockSpec((rows, inner), lambda i: (0, 0))] * NZ
        + [pl.BlockSpec((NY, tokens, inner), lambda i: (0, 0, 0))] * NC,
        out_shape=[
            jax.ShapeDtypeStruct((rows, inner), BF16 if dz else F32) for dz in range(NZ)
        ]
        + [jax.ShapeDtypeStruct((NY, tokens, inner), F32)] * NC,
        scratch_shapes=[
            pltpu.VMEM((PLANE * tokens, inner), BF16),
            pltpu.VMEM((PLANE * tokens, block), BF16),
        ],
        compiler_params=roomy(),
        cost_estimate=cost(
            4 * PLANE * tokens * inner * block,
            2 * PLANE * tokens * (3 * inner + block) + 2 * block * inner,
        ),
        name="weight_and_value_terms",
    )(same, other, first, second, *[hidden] * PLANE)


def input_grad_kernel(
    x_ref, gain_ref, scale_ref, grad_hbm, out_hbm, grad_ref, out_ref, grad_sems, out_sems
):
    tokens, width = x_ref.shape
    rows = width // (NZ * PLANE)
    steps = grad_sems.shape[0]
    step = tokens // steps
    tile = step // out_sems.shape[1]
    half = PLANE // 2

    def fetches(i):
        at = pl.ds(i * step, step)
        copies = []
        for part in range(2):
            members = pl.ds(part * half, half)
            copies.append(
                pltpu.make_async_copy(
                    grad_hbm.at[members, at], grad_ref.at[members, at], grad_sems.at[i, part]
                )
            )
        return copies

    def stores(i):
        copies = []
        for part in range(step // tile):
            at = pl.ds(i * step + part * tile, tile)
            copies.append(
                pltpu.make_async_copy(out_ref.at[at], out_hbm.at[at], out_sems.at[i, part])
            )
        return copies

    for i in range(steps):
        for copy in fetches(i):
            copy.start()
    for i in range(steps):
        for copy in fetches(i):
            copy.wait()
        here = slice(i * step, (i + 1) * step)
        scale = scale_ref[here]
        total = jnp.zeros((step, rows), F32)
        for dz in range(NZ):
            for member in range(PLANE):
                at = pl.ds(feature_start(member, dz, rows), rows)
                grad = grad_ref[member, here, dz * rows : (dz + 1) * rows]
                scaled = grad.astype(F32) * gain_ref[:, at]
                out_ref[here, at] = scaled
                total += scaled * x_ref[here, at].astype(F32)
        mean = scale * jnp.sum(total, axis=-1, keepdims=True) * (1.0 / width)
        factor = scale * scale * mean
        for block in range(NZ * PLANE):
            at = slice(block * rows, (block + 1) * rows)
            out_ref[here, at] = scale * out_ref[here, at] - x_ref[here, at].astype(F32) * factor
        for copy in stores(i):
            copy.start()
    for i in range(steps):
        for copy in stores(i):
            copy.wait()


def make_input_grad(inputs, gain, scale, grads):
    tokens, width = inputs.shape
    steps = 4
    hbm, vmem = pl.BlockSpec(memory_space=pltpu.HBM), pl.BlockSpec(memory_space=pltpu.VMEM)
    return pl.pallas_call(
        input_grad_kernel,
        in_specs=[vmem, vmem, vmem, hbm],
        out_specs=hbm,
        out_shape=jax.ShapeDtypeStruct((tokens, width), F32),
        scratch_shapes=[
            pltpu.VMEM(grads.shape, grads.dtype),
            pltpu.VMEM((tokens, width), F32),
            pltpu.SemaphoreType.DMA((steps, 2)),
            pltpu.SemaphoreType.DMA((steps, 4)),
        ],
        compiler_params=roomy(24),
        cost_estimate=cost(9 * tokens * width, 8 * tokens * width),
        name="input_grad",
    )(inputs, gain, scale, grads)


def sum_over_x(delta):
    width = delta.shape[1] // 4
    x = lax.axis_index("rep") // 2
    total = lax.dynamic_slice_in_dim(delta, x * width, width, 1)
    for dx in (2, 1, 3):
        piece = lax.dynamic_slice_in_dim(delta, (x ^ dx) * width, width, 1)
        total = total + swap(piece.astype(BF16), "rep", 2 * dx).astype(F32)
    return total


def sum_over_halves(delta):
    width = delta.shape[1] // 2
    half = lax.axis_index("rep") % 2
    give = lax.dynamic_slice_in_dim(delta, (1 - half) * width, width, 1)
    return lax.dynamic_slice_in_dim(delta, half * width, width, 1) + swap(give, "rep", 1)


def outer_step(total, params, moment):
    average = total / lax.axis_size("rep")
    new_moment = 0.9 * moment + average
    new_params = params - 0.7 * (average + 0.9 * new_moment)
    return new_params, new_moment


def gather_pairs(array, bits):
    array = jnp.concatenate([array, swap(array, "fsdp", 2 * bits)], axis=0)
    return array, swap(array, "fsdp", bits)


def shards(inputs, cotangent, value_weight, norm_gain, outer_delta, outer_params, outer_moment):
    index = lax.axis_index("fsdp")
    gain = norm_gain.reshape(1, -1)
    rows = value_weight.shape[0]

    first = jnp.concatenate([value_weight, swap(value_weight, "fsdp", 2 * PLANE)], axis=0)
    same = jnp.concatenate(
        [cotangent] + [swap(cotangent, "fsdp", dy * NC) for dy in HALVES[1:]], axis=0
    )
    scale, blocks = make_hidden(inputs, gain)
    blocks, same, first = together(blocks, same, first)

    hidden = exchange_plane(blocks)
    second = swap(first, "fsdp", PLANE)
    other = swap(same, "fsdp", 1)
    own_gain = lax.dynamic_slice_in_dim(norm_gain, index * rows, rows, 0)
    weight_by_gain = value_weight.astype(F32) / own_gain[:, None]
    delta = sum_over_x(outer_delta)
    same, delta = together(same, delta)
    delta = sum_over_halves(delta)
    new_params, new_moment = outer_step(delta, outer_params, outer_moment)
    grads = make_hidden_grad(same, other, first, second)
    hidden, new_moment, weight_by_gain = together(hidden, new_moment, weight_by_gain)
    back = exchange_plane(grads)

    *terms, keep, give = make_terms(same, other, first, second, hidden)
    got = [swap(terms[dz], "fsdp", dz * PLANE) for dz in (1, 2, 3)]
    (pair,) = together(keep + swap(give, "fsdp", 1))
    back, values = together(back, pair[0])
    parts = [swap(pair[dy].astype(BF16), "fsdp", dy * NC) for dy in (1, 2, 3)]
    input_grad = make_input_grad(inputs, gain, scale, back)
    input_grad, *got = together(input_grad, *got)
    input_grad, *parts = together(input_grad, *parts)
    for part in parts:
        values = values + part.astype(F32)
    weight_sum = terms[0]
    for part in got:
        weight_sum = weight_sum + part.astype(F32)
    scale_grad = 1.0 / math.sqrt(inputs.shape[0] * lax.axis_size("fsdp"))
    weight_grad = weight_sum * scale_grad
    gain_grad = jnp.sum(weight_grad * weight_by_gain, axis=1)
    return values, input_grad, weight_grad, gain_grad, new_params, new_moment


def solution(mesh):
    rows = P(("rep", "fsdp"), None)
    in_specs = (rows, rows, rows, P("rep"), rows, P("fsdp", "rep"), P("fsdp", "rep"))
    out_specs = (rows, rows, rows, P(("rep", "fsdp")), P("fsdp", "rep"), P("fsdp", "rep"))
    return jax.shard_map(shards, mesh=mesh, in_specs=in_specs, out_specs=out_specs, check_vma=False)
```
